256 devices in a mesh: img: 16 (over y_lo, x, core), slab: 16 (over z, y_hi).
Axes of the slice: x: 4, y: 4 (y_hi: 2, y_lo: 2; y = y_hi * 2 + y_lo), z: 8, core: 2. Of those that a mesh axis runs over, the one named last changes fastest.
Arguments:
- state: float32 [128, 2, 512, 4, 128], P('img', None, 'slab'), may hold values from -3 to 3
- sources: int32 [128, 2], replicated, may hold values from 0 to 127, as said below
- weight_index: int32 [128], P('img'), may hold values from 0 to 15
Outputs:
- moved: float32 [128, 2, 512, 4, 128], P('img', None, 'slab')
The draws below stay inside these ranges and needn't reach their ends.
Inputs may be any that keep to these rules, and one draw needn't show every extreme that they name: Among the 16 sources of the 8 new images of one device (aligned blocks), at most 2 lie among the 8 images of any one device, and in every draw exactly 2 do for some devices.
All inputs are finite; a program needn't handle non-finite values.
Results may differ from the reference program's by a relative error of at most 0.00022.
Values sent between devices are 32-bit elements; how exact they have to be, the bound alone decides.
No kernel may reach another device: no remote copies, remote signals or barrier semaphores. Data moves between devices by JAX's collectives and lax.ppermute only.
A program may use at most 128 MiB of HBM per device.

```python
import jax
import jax.numpy as jnp
from jax import lax

IMG_DEV = 8
GX = 4
GY = 128
SLOTS = 2
WLEVELS = 16
IMAGES = 128
NZ = 512


def draw_sources(key, part):
    key = jax.random.fold_in(key, 11)
    blocks = IMAGES // IMG_DEV
    entries = 2 * IMG_DEV
    subkeys = jax.random.split(key, blocks)

    def one_block(subkey):
        first_key, second_key, third_key = jax.random.split(subkey, 3)
        senders = jax.random.permutation(first_key, blocks)
        positions = jnp.arange(entries, dtype=jnp.int32)
        picks = positions // SLOTS
        ordering = jax.random.permutation(second_key, entries)
        owners = senders[picks[ordering]]
        offsets = jax.random.randint(third_key, (entries,), 0, IMG_DEV)
        return (owners * IMG_DEV + offsets).astype(jnp.int32)
    return jax.vmap(one_block)(subkeys).reshape(IMAGES, 2)


def plant(drawn, key, least, largest):
    shape = drawn.shape
    index_at = [jax.random.randint(jax.random.fold_in(key, axis), (), 0, shape[axis]) for axis in range(len(shape))]
    drawn = drawn.at[tuple(index_at)].set(least)
    longest = shape.index(max(shape))
    index_at[longest] = (index_at[longest] + 1) % shape[longest]
    return drawn.at[tuple(index_at)].set(largest)


def block_scale(key, dims, cuts, least, high):
    factor_of = 1.0
    for dim, shards_of in cuts:
        draws = jax.random.uniform(jax.random.fold_in(jax.random.fold_in(key, 6), dim), (shards_of,), jnp.float32, least / len(cuts), high / len(cuts))
        factor_of = factor_of * jnp.repeat(jnp.exp(draws), dims[dim] // shards_of).reshape((-1,) + (1,) * (len(dims) - 1 - dim))
    return factor_of


def bell_draw(stream_key, dims, width, bound, cuts=(), kind=jnp.bfloat16):
    gain = block_scale(stream_key, dims, cuts, -0.22, 0.18) if cuts else 1.0
    values = jax.random.normal(stream_key, dims, jnp.float32) * width * gain
    return jnp.minimum(jnp.maximum(values, -bound), bound).astype(kind)


def setup_inputs(seed: int = 0) -> dict:
    keys = jax.random.split(jax.random.key(seed), 4)
    state = bell_draw(keys[0], (IMAGES, 2, NZ, GX, GY), 0.5, 3.0, ((0, 16), (2, 16)), jnp.float32)
    sources = draw_sources(jax.random.fold_in(keys[3], 71), 0)
    weight_index = plant(jax.random.randint(keys[2], (IMAGES,), 0, WLEVELS), jax.random.fold_in(keys[2], 1), 0, WLEVELS - 1).astype(jnp.int32)
    return dict(state=state, sources=sources, weight_index=weight_index)


KAPPA = 0.25
COUPLE = 0.3
STEP_SIZE = 0.004
EPSILON = 1e-06

def drift(phi, face):
    padded = jnp.pad(phi, ((0, 0), (1, 1), (0, 0), (0, 0)))
    lapl = padded[:, 2:] + padded[:, :-2]
    lapl = lapl + jnp.roll(phi, 1, 2) + jnp.roll(phi, -1, 2)
    lapl = lapl + jnp.roll(phi, 1, 3) + jnp.roll(phi, -1, 3) - 6.0 * phi
    potential = phi * phi * phi - phi + COUPLE * phi[::-1] - KAPPA * lapl
    mobile = 0.5 + 1.0 / (1.0 + phi * phi)
    total = jnp.zeros_like(phi)
    for axis_no in (2, 3):
        face_mob = 0.5 * (mobile + jnp.roll(mobile, -1, axis_no))
        flux = face_mob * (jnp.roll(potential, -1, axis_no) - potential)
        total = total + flux - jnp.roll(flux, 1, axis_no)
    face_z = 0.5 * (mobile[:, 1:] + mobile[:, :-1]) * face[None, :, None, None]
    flux_z = face_z * (potential[:, 1:] - potential[:, :-1])
    total = total + jnp.pad(flux_z, ((0, 0), (0, 1), (0, 0), (0, 0)))
    total = total - jnp.pad(flux_z, ((0, 0), (1, 0), (0, 0), (0, 0)))
    return total

def reference(state, sources, weight_index):
    images = state.shape[0]
    face = jnp.ones((state.shape[2] - 1,), jnp.float32)

    def update(index):
        before = lax.dynamic_index_in_dim(state, index - 1, 0, keepdims=False)
        current = lax.dynamic_index_in_dim(state, index, 0, keepdims=False)
        after = lax.dynamic_index_in_dim(state, index + 1, 0, keepdims=False)
        own_drift = drift(current, face)
        tangent = (after - before) * ((images - 1) / 2.0)
        second = (after - 2.0 * current + before) * float((images - 1) ** 2)
        scale = jnp.sqrt(jnp.sum(own_drift * own_drift)) / jnp.sqrt(jnp.sum(tangent * tangent) + EPSILON)
        moment = scale * tangent - own_drift
        _, back = jax.vjp(lambda field: drift(field, face), current)
        pulled = back(moment)[0]
        return current + STEP_SIZE * (scale * scale * second + pulled)
    inner = lax.map(update, jnp.arange(1, images - 1, dtype=jnp.int32))
    updated = jnp.concatenate([state[:1], inner, state[-1:]], axis=0)
    weights = (weight_index.astype(jnp.float32) + 1.0) / (WLEVELS + 1.0)

    def place(index):
        first = lax.dynamic_index_in_dim(updated, sources[index, 0], 0, keepdims=False)
        other = lax.dynamic_index_in_dim(updated, sources[index, 1], 0, keepdims=False)
        weight = weights[index]
        return weight * first + (1.0 - weight) * other
    return lax.map(place, jnp.arange(images, dtype=jnp.int32))
```

```python
import functools

import jax
import jax.numpy as jnp
from jax import lax
from jax.experimental import pallas as pl
from jax.experimental.pallas import tpu as pltpu
from jax.sharding import PartitionSpec as P

WLEVELS = 16
KAPPA = 0.25
COUPLE = 0.3
STEP_SIZE = 0.004
EPSILON = 1e-06

F32 = jnp.float32
HALO = 4
GX = 4
LIMIT = 24 * 1024 * 1024


def turn(value, shift):
    return pltpu.roll(value, shift % 128, 1)


def face_open(z, total):
    return jnp.where((z >= 0) & (z + 1 < total), 1.0, 0.0).astype(F32)


def drift_kernel(total, depth, place, body, side_a, side_b, ext, mu, half, own, squares, sems):
    copies = [
        pltpu.make_async_copy(body, ext.at[:, pl.ds(HALO, depth)], sems.at[0]),
        pltpu.make_async_copy(side_a, ext.at[:, pl.ds(place[1], HALO)], sems.at[1]),
        pltpu.make_async_copy(side_b, ext.at[:, pl.ds(place[2], HALO)], sems.at[2]),
    ]
    for copy in copies:
        copy.start()
    for copy in copies:
        copy.wait()
    zero = place[0] - HALO

    def potential(e, carry):
        here = [[ext[f, e, x] for x in range(GX)] for f in range(2)]
        for f in range(2):
            for x in range(GX):
                phi = here[f][x]
                around = ext[f, e - 1, x] + ext[f, e + 1, x]
                around = around + (here[f][(x + 1) % GX] + here[f][(x - 1) % GX])
                around = around + (turn(phi, 1) + turn(phi, -1))
                square = phi * phi
                mu[f, e, x] = phi * (square + (6.0 * KAPPA - 1.0)) + COUPLE * here[1 - f][x] - KAPPA * around
                half[f, e, x] = 0.25 + 0.5 / (1.0 + square)
        return carry

    lax.fori_loop(1, depth + 2 * HALO - 1, potential, 0)

    def face_z(e, f, x):
        return (half[f, e, x] + half[f, e + 1, x]) * (mu[f, e + 1, x] - mu[f, e, x])

    def flux(e, carry):
        lower, acc = carry
        is_open = face_open(zero + e, total)
        counted = jnp.where((e >= HALO) & (e < depth + HALO), 1.0, 0.0).astype(F32)
        upper = []
        for f in range(2):
            m = [mu[f, e, x] for x in range(GX)]
            h = [half[f, e, x] for x in range(GX)]
            side = [(h[x] + h[(x + 1) % GX]) * (m[(x + 1) % GX] - m[x]) for x in range(GX)]
            for x in range(GX):
                along = (h[x] + turn(h[x], -1)) * (turn(m[x], -1) - m[x])
                up = face_z(e, f, x) * is_open
                value = (side[x] - side[(x - 1) % GX]) + (along - turn(along, 1)) + (up - lower[f * GX + x])
                own[f, e, x] = value
                acc = acc + value * value * counted
                upper.append(up)
        return tuple(upper), acc

    first = face_open(zero + 1, total)
    lower = tuple(face_z(1, f, x) * first for f in range(2) for x in range(GX))
    _, acc = lax.fori_loop(2, depth + 2 * HALO - 2, flux, (lower, jnp.zeros((8, 128), F32)))
    squares[...] = acc


def neighbours(ext, before, after, e, f, x, rows):
    index = (f * rows + (e - 2)) * GX + x
    here = ext[f, e, x]
    sub = lax.broadcasted_iota(jnp.int32, (8, 128), 0)
    prev = jnp.where(sub == 0, before[pl.ds(index, 1), :], pltpu.roll(here, 1, 0))
    following = jnp.where(sub == 7, after[pl.ds(index, 1), :], pltpu.roll(here, 7, 0))
    return here, prev, following


def sums_kernel(depth, ext, before, after, squares, sums):
    def step(e, acc):
        for f in range(2):
            for x in range(GX):
                _, prev, following = neighbours(ext, before, after, e, f, x, depth + 4)
                d = following - prev
                acc = acc + d * d
        return acc

    acc = lax.fori_loop(HALO, depth + HALO, step, jnp.zeros((8, 128), F32))
    sub = lax.broadcasted_iota(jnp.int32, (8, 128), 0)
    lane = lax.broadcasted_iota(jnp.int32, (8, 128), 1)
    drift_sq = jnp.sum(squares[...], axis=1, keepdims=True)
    tangent_sq = jnp.sum(acc, axis=1, keepdims=True)
    row = jnp.where(lane == sub, drift_sq, jnp.where(lane == sub + 8, tangent_sq, 0.0))
    sums[...] = jnp.broadcast_to(jnp.sum(row, axis=0, keepdims=True), sums.shape)


def update_kernel(total, depth, images, place, ext, before, after, mu, half, own, sums, weight, out, m_ref, bar, inner):
    zero = place[0] - HALO
    sub = lax.broadcasted_iota(jnp.int32, (8, 128), 0)
    lane = lax.broadcasted_iota(jnp.int32, (8, 128), 1)
    added = jnp.sum(sums[...], axis=0, keepdims=True)
    drift_sq = jnp.sum(jnp.where(lane == sub, added, 0.0), axis=1, keepdims=True)
    tangent_sq = jnp.sum(jnp.where(lane == sub + 8, added, 0.0), axis=1, keepdims=True)
    rate = (images - 1) / 2.0
    scale = jnp.sqrt(drift_sq) / jnp.sqrt(tangent_sq * (rate * rate) + EPSILON)
    by_tangent = jnp.broadcast_to(scale * rate, (8, 128))
    by_second = jnp.broadcast_to(scale * scale * float((images - 1) ** 2), (8, 128))
    index = place[3] + sub
    step_size = jnp.where((index > 0) & (index < images - 1), STEP_SIZE, 0.0).astype(F32)

    def momentum(e, carry):
        for f in range(2):
            for x in range(GX):
                _, prev, following = neighbours(ext, before, after, e, f, x, depth + 4)
                m_ref[f, e, x] = by_tangent * (following - prev) - own[f, e, x]
        return carry

    lax.fori_loop(2, depth + 2 * HALO - 2, momentum, 0)

    def face_z(e, f, x, is_open):
        dm = m_ref[f, e + 1, x] - m_ref[f, e, x]
        dmu = mu[f, e + 1, x] - mu[f, e, x]
        g = (half[f, e, x] + half[f, e + 1, x]) * dm * is_open
        return g, dm * dmu * is_open

    def adjoint(e, carry):
        is_open = face_open(zero + e, total)
        inside = jnp.where((zero + e >= 0) & (zero + e < total), 1.0, 0.0).astype(F32)
        upper = []
        for f in range(2):
            m = [m_ref[f, e, x] for x in range(GX)]
            p = [mu[f, e, x] for x in range(GX)]
            h = [half[f, e, x] for x in range(GX)]
            side = []
            for x in range(GX):
                n = (x + 1) % GX
                dm = m[n] - m[x]
                side.append(((h[x] + h[n]) * dm, dm * (p[n] - p[x])))
            for x in range(GX):
                dm = turn(m[x], -1) - m[x]
                g_y = (h[x] + turn(h[x], -1)) * dm
                q_y = dm * (turn(p[x], -1) - p[x])
                g_z, q_z = face_z(e, f, x, is_open)
                g_low, q_low = carry[f * GX + x]
                b = (x - 1) % GX
                g = (side[x][0] - side[b][0]) + (g_y - turn(g_y, 1)) + (g_z - g_low)
                q = (side[x][1] + side[b][1]) + (q_y + turn(q_y, 1)) + (q_z + q_low)
                bar[f, e, x] = g * inside
                inner[f, e, x] = q
                upper.append((g_z, q_z))
        return tuple(upper)

    first = face_open(zero + 2, total)
    lax.fori_loop(
        3,
        depth + 2 * HALO - 3,
        adjoint,
        tuple(face_z(2, f, x, first) for f in range(2) for x in range(GX)),
    )

    def finish(r, carry):
        for zz in range(2):
            e = 2 * r + zz + HALO
            for f in range(2):
                g = [bar[f, e, x] for x in range(GX)]
                for x in range(GX):
                    phi, prev, following = neighbours(ext, before, after, e, f, x, depth + 4)
                    around = bar[f, e - 1, x] + bar[f, e + 1, x]
                    around = around + (g[(x + 1) % GX] + g[(x - 1) % GX])
                    around = around + (turn(g[x], 1) + turn(g[x], -1))
                    inverse = 2.0 * half[f, e, x] - 0.5
                    pulled = phi * (inverse * inverse) * inner[f, e, x]
                    pulled = pulled + (3.0 * (phi * phi) + (6.0 * KAPPA - 1.0)) * g[x]
                    pulled = pulled + COUPLE * bar[1 - f, e, x] - KAPPA * around
                    second = (following - phi) + (prev - phi)
                    out[r, f * 2 * GX + zz * GX + x] = phi + step_size * (by_second * second + pulled)
        out[r, 4 * GX] = weight[...]
        return carry

    lax.fori_loop(0, depth // 2, finish, 0)


def mix_kernel(images, rows, sources, got, out):
    block = (rows + 1) * 8

    def step(j, carry):
        first, other = sources[j, 0], sources[j, 1]
        a = (first // 8) * block + first % 8
        b = (other // 8) * block + other % 8
        w = got[pl.ds((j // 8) * block + rows * 8 + j % 8, 1), :]
        for part in range(rows // 8):
            one = got[pl.ds(a + part * 64, 8, stride=8), :]
            two = got[pl.ds(b + part * 64, 8, stride=8), :]
            out[pl.ds(pl.multiple_of(j * rows + part * 8, 8), 8), :] = w * one + (1.0 - w) * two
        return carry

    lax.fori_loop(0, images, step, 0)


ANY = pl.BlockSpec(memory_space=pl.ANY)
VMEM = pl.BlockSpec(memory_space=pltpu.VMEM)
SMEM = pl.BlockSpec(memory_space=pltpu.SMEM)


def call(kernel, ins, in_specs, outs, scratch=(), flops=0, moved=0):
    return pl.pallas_call(
        kernel,
        in_specs=in_specs,
        out_specs=jax.tree.map(lambda _: VMEM, outs),
        out_shape=outs,
        scratch_shapes=list(scratch),
        compiler_params=pltpu.CompilerParams(vmem_limit_bytes=LIMIT),
        cost_estimate=pl.CostEstimate(flops=flops, bytes_accessed=moved, transcendentals=0),
    )(*ins)


def swaps(count):
    near = [(i, i ^ 1) for i in range(count)]
    far = [pair for i in range(1, count - 1, 2) for pair in ((i, i + 1), (i + 1, i))]
    return near, far


def local(state, sources, weight_index):
    img_count, slab_count = lax.axis_size("img"), lax.axis_size("slab")
    img_rank, slab_rank = lax.axis_index("img"), lax.axis_index("slab")
    per_dev, _, depth, _, _ = state.shape
    images, total = per_dev * img_count, depth * slab_count
    even_img, even_slab = img_rank % 2 == 0, slab_rank % 2 == 0

    body = state.transpose(1, 2, 3, 0, 4)
    top, bottom = body[:, -HALO:], body[:, :HALO]
    near, far = swaps(slab_count)
    side_a = lax.ppermute(jnp.where(even_slab, top, bottom), "slab", near)
    side_b = lax.ppermute(jnp.where(even_slab, bottom, top), "slab", far)

    low = jnp.where(even_slab, side_b, side_a)[:, 2:]
    high = jnp.where(even_slab, side_a, side_b)[:, :2]
    ends = [
        jnp.concatenate([low[:, :, :, i], body[:, :, :, i], high[:, :, :, i]], axis=1).reshape(-1, 128)
        for i in (0, per_dev - 1)
    ]
    near, far = swaps(img_count)
    image_a = lax.ppermute(jnp.where(even_img, ends[1], ends[0]), "img", near)
    image_b = lax.ppermute(jnp.where(even_img, ends[0], ends[1]), "img", far)
    before = jnp.where(even_img, image_b, image_a)
    after = jnp.where(even_img, image_a, image_b)

    place = jnp.stack(
        [
            slab_rank * depth,
            jnp.where(even_slab, depth + HALO, 0),
            jnp.where(even_slab, 0, depth + HALO),
            img_rank * per_dev,
        ]
    ).astype(jnp.int32)
    wide = jax.ShapeDtypeStruct((2, depth + 2 * HALO, GX, 8, 128), F32)
    tile = jax.ShapeDtypeStruct((8, 128), F32)
    ext, mu, half, own, squares = call(
        functools.partial(drift_kernel, total, depth),
        (place, body, side_a, side_b),
        [SMEM, ANY, ANY, ANY],
        [wide, wide, wide, wide, tile],
        [pltpu.SemaphoreType.DMA((3,))],
        flops=20_000_000,
        moved=8_000_000,
    )
    sums = call(
        functools.partial(sums_kernel, depth),
        (ext, before, after, squares),
        [VMEM] * 4,
        jax.ShapeDtypeStruct((slab_count, 128), F32),
    )
    sums = lax.all_to_all(sums, "slab", 0, 0, tiled=True)
    weight = jnp.broadcast_to(((weight_index.astype(F32) + 1.0) / (WLEVELS + 1.0))[:, None], (8, 128))
    rows = 4 * GX
    updated = call(
        functools.partial(update_kernel, total, depth, images),
        (place, ext, before, after, mu, half, own, sums, weight),
        [SMEM] + [VMEM] * 8,
        jax.ShapeDtypeStruct((depth // 2, rows + 1, 8, 128), F32),
        [pltpu.VMEM(wide.shape, F32)] * 3,
    )
    got = lax.all_to_all(updated, "img", 0, 0, tiled=True)
    new = call(
        functools.partial(mix_kernel, images, rows),
        (sources, got.reshape(-1, 128)),
        [SMEM, VMEM],
        jax.ShapeDtypeStruct((images * rows, 128), F32),
    )
    new = lax.all_to_all(new.reshape(img_count, per_dev, 2, 2, GX, 128), "img", 0, 0, tiled=True)
    return new.transpose(1, 2, 0, 3, 4, 5).reshape(state.shape)


def solution(mesh):
    return jax.shard_map(
        local,
        mesh=mesh,
        in_specs=(P("img", None, "slab", None, None), P(), P("img")),
        out_specs=P("img", None, "slab", None, None),
        check_vma=False,
    )
```

```python
import functools

import jax
import jax.numpy as jnp
from jax import lax
from jax.experimental import pallas as pl
from jax.experimental.pallas import tpu as pltpu
from jax.sharding import PartitionSpec as P

WLEVELS = 16
KAPPA = 0.25
COUPLE = 0.3
STEP_SIZE = 0.004
EPSILON = 1e-06

F32 = jnp.float32
HALO = 4
GX = 4
LIMIT = 8 * 1024 * 1024
U1, U2, U3, U4, U5, U6, U7 = 2, 4, 4, 4, 2, 1, 8


def turn(value, shift):
    return pltpu.roll(value, shift % 128, 1)


def recip(d):
    r = pltpu.reciprocal(d, approx=True)
    r = r * (2.0 - d * r)
    return r * (2.0 - d * r)


def face_open(z, total):
    return jnp.where((z >= 0) & (z + 1 < total), 1.0, 0.0).astype(F32)


def drift_kernel(total, depth, place, body, side_a, side_b, ext, mu, half, own, squares, sems):
    copies = [
        pltpu.make_async_copy(body, ext.at[:, pl.ds(HALO, depth)], sems.at[0]),
        pltpu.make_async_copy(side_a, ext.at[:, pl.ds(place[1], HALO)], sems.at[1]),
        pltpu.make_async_copy(side_b, ext.at[:, pl.ds(place[2], HALO)], sems.at[2]),
    ]
    for copy in copies:
        copy.start()
    for copy in copies:
        copy.wait()
    zero = place[0] - HALO

    def potential(e, carry):
        here = [[ext[f, e, x] for x in range(GX)] for f in range(2)]
        for f in range(2):
            for x in range(GX):
                phi = here[f][x]
                around = ext[f, e - 1, x] + ext[f, e + 1, x]
                around = around + (here[f][(x + 1) % GX] + here[f][(x - 1) % GX])
                around = around + (turn(phi, 1) + turn(phi, -1))
                square = phi * phi
                mu[f, e, x] = phi * (square + (6.0 * KAPPA - 1.0)) + COUPLE * here[1 - f][x] - KAPPA * around
                half[f, e, x] = 0.25 + 0.5 * recip(1.0 + square)
        return carry

    lax.fori_loop(1, depth + 2 * HALO - 1, potential, 0, unroll=U1)

    def face_z(e, f, x):
        return (half[f, e, x] + half[f, e + 1, x]) * (mu[f, e + 1, x] - mu[f, e, x])

    def flux(e, carry):
        lower, acc = carry
        is_open = face_open(zero + e, total)
        counted = jnp.where((e >= HALO) & (e < depth + HALO), 1.0, 0.0).astype(F32)
        upper = []
        for f in range(2):
            m = [mu[f, e, x] for x in range(GX)]
            h = [half[f, e, x] for x in range(GX)]
            side = [(h[x] + h[(x + 1) % GX]) * (m[(x + 1) % GX] - m[x]) for x in range(GX)]
            for x in range(GX):
                along = (h[x] + turn(h[x], -1)) * (turn(m[x], -1) - m[x])
                up = face_z(e, f, x) * is_open
                value = (side[x] - side[(x - 1) % GX]) + (along - turn(along, 1)) + (up - lower[f * GX + x])
                own[f, e, x] = value
                acc = acc + value * value * counted
                upper.append(up)
        return tuple(upper), acc

    first = face_open(zero + 1, total)
    lower = tuple(face_z(1, f, x) * first for f in range(2) for x in range(GX))
    _, acc = lax.fori_loop(2, depth + 2 * HALO - 2, flux, (lower, jnp.zeros((8, 128), F32)), unroll=U2)
    squares[...] = acc


def neighbours(ext, before, after, e, f, x, rows):
    index = (f * rows + (e - 2)) * GX + x
    here = ext[f, e, x]
    sub = lax.broadcasted_iota(jnp.int32, (8, 128), 0)
    prev = jnp.where(sub == 0, before[pl.ds(index, 1), :], pltpu.roll(here, 1, 0))
    following = jnp.where(sub == 7, after[pl.ds(index, 1), :], pltpu.roll(here, 7, 0))
    return here, prev, following


def sums_kernel(depth, ext, before, after, squares, sums):
    def step(e, acc):
        for f in range(2):
            for x in range(GX):
                _, prev, following = neighbours(ext, before, after, e, f, x, depth + 4)
                d = following - prev
                acc = acc + d * d
        return acc

    acc = lax.fori_loop(HALO, depth + HALO, step, jnp.zeros((8, 128), F32), unroll=U3)
    sub = lax.broadcasted_iota(jnp.int32, (8, 128), 0)
    lane = lax.broadcasted_iota(jnp.int32, (8, 128), 1)
    drift_sq = jnp.sum(squares[...], axis=1, keepdims=True)
    tangent_sq = jnp.sum(acc, axis=1, keepdims=True)
    row = jnp.where(lane == sub, drift_sq, jnp.where(lane == sub + 8, tangent_sq, 0.0))
    sums[...] = jnp.broadcast_to(jnp.sum(row, axis=0, keepdims=True), sums.shape)


def update_kernel(total, depth, images, place, ext, before, after, mu, half, own, sums, weight, out, m_ref, bar, inner):
    zero = place[0] - HALO
    sub = lax.broadcasted_iota(jnp.int32, (8, 128), 0)
    lane = lax.broadcasted_iota(jnp.int32, (8, 128), 1)
    added = jnp.sum(sums[...], axis=0, keepdims=True)
    drift_sq = jnp.sum(jnp.where(lane == sub, added, 0.0), axis=1, keepdims=True)
    tangent_sq = jnp.sum(jnp.where(lane == sub + 8, added, 0.0), axis=1, keepdims=True)
    rate = (images - 1) / 2.0
    scale = jnp.sqrt(drift_sq) / jnp.sqrt(tangent_sq * (rate * rate) + EPSILON)
    by_tangent = jnp.broadcast_to(scale * rate, (8, 128))
    by_second = jnp.broadcast_to(scale * scale * float((images - 1) ** 2), (8, 128))
    index = place[3] + sub
    step_size = jnp.where((index > 0) & (index < images - 1), STEP_SIZE, 0.0).astype(F32)

    def momentum(e, carry):
        for f in range(2):
            for x in range(GX):
                _, prev, following = neighbours(ext, before, after, e, f, x, depth + 4)
                m_ref[f, e, x] = by_tangent * (following - prev) - own[f, e, x]
        return carry

    lax.fori_loop(2, depth + 2 * HALO - 2, momentum, 0, unroll=U4)

    def face_z(e, f, x, is_open):
        dm = m_ref[f, e + 1, x] - m_ref[f, e, x]
        dmu = mu[f, e + 1, x] - mu[f, e, x]
        g = (half[f, e, x] + half[f, e + 1, x]) * dm * is_open
        return g, dm * dmu * is_open

    def adjoint(e, carry):
        is_open = face_open(zero + e, total)
        inside = jnp.where((zero + e >= 0) & (zero + e < total), 1.0, 0.0).astype(F32)
        upper = []
        for f in range(2):
            m = [m_ref[f, e, x] for x in range(GX)]
            p = [mu[f, e, x] for x in range(GX)]
            h = [half[f, e, x] for x in range(GX)]
            side = []
            for x in range(GX):
                n = (x + 1) % GX
                dm = m[n] - m[x]
                side.append(((h[x] + h[n]) * dm, dm * (p[n] - p[x])))
            for x in range(GX):
                dm = turn(m[x], -1) - m[x]
                g_y = (h[x] + turn(h[x], -1)) * dm
                q_y = dm * (turn(p[x], -1) - p[x])
                g_z, q_z = face_z(e, f, x, is_open)
                g_low, q_low = carry[f * GX + x]
                b = (x - 1) % GX
                g = (side[x][0] - side[b][0]) + (g_y - turn(g_y, 1)) + (g_z - g_low)
                q = (side[x][1] + side[b][1]) + (q_y + turn(q_y, 1)) + (q_z + q_low)
                bar[f, e, x] = g * inside
                inner[f, e, x] = q
                upper.append((g_z, q_z))
        return tuple(upper)

    first = face_open(zero + 2, total)
    lax.fori_loop(
        3,
        depth + 2 * HALO - 3,
        adjoint,
        tuple(face_z(2, f, x, first) for f in range(2) for x in range(GX)),
        unroll=U5,
    )

    def finish(r, carry):
        for zz in range(2):
            e = 2 * r + zz + HALO
            for f in range(2):
                g = [bar[f, e, x] for x in range(GX)]
                for x in range(GX):
                    phi, prev, following = neighbours(ext, before, after, e, f, x, depth + 4)
                    around = bar[f, e - 1, x] + bar[f, e + 1, x]
                    around = around + (g[(x + 1) % GX] + g[(x - 1) % GX])
                    around = around + (turn(g[x], 1) + turn(g[x], -1))
                    inverse = 2.0 * half[f, e, x] - 0.5
                    pulled = phi * (inverse * inverse) * inner[f, e, x]
                    pulled = pulled + (3.0 * (phi * phi) + (6.0 * KAPPA - 1.0)) * g[x]
                    pulled = pulled + COUPLE * bar[1 - f, e, x] - KAPPA * around
                    second = (following - phi) + (prev - phi)
                    out[r, pl.ds(f * 2 * GX + zz * GX + x, 8, stride=4 * GX), :] = phi + step_size * (by_second * second + pulled)
        out[r, pl.ds(32 * GX, 8), :] = weight[...]
        return carry

    lax.fori_loop(0, depth // 2, finish, 0, unroll=U6)


def mix_kernel(images, rows, starts, got, out):
    block = (rows + 1) * 8

    def step(j, carry):
        a = pl.multiple_of(starts[j], 8)
        b = pl.multiple_of(starts[images + j], 8)
        w = got[pl.ds((j // 8) * block + rows * 8 + j % 8, 1), :]
        for part in range(0, rows, 8):
            one, two = got[pl.ds(a + part, 8), :], got[pl.ds(b + part, 8), :]
            out[pl.ds(pl.multiple_of(j * rows + part, 8), 8), :] = w * one + (1.0 - w) * two
        return carry

    lax.fori_loop(0, images, step, 0, unroll=U7)


ANY = pl.BlockSpec(memory_space=pl.ANY)
VMEM = pl.BlockSpec(memory_space=pltpu.VMEM)
SMEM = pl.BlockSpec(memory_space=pltpu.SMEM)


def call(kernel, ins, in_specs, outs, scratch=(), flops=0, moved=0):
    return pl.pallas_call(
        kernel,
        in_specs=in_specs,
        out_specs=jax.tree.map(lambda _: VMEM, outs),
        out_shape=outs,
        scratch_shapes=list(scratch),
        compiler_params=pltpu.CompilerParams(vmem_limit_bytes=LIMIT),
        cost_estimate=pl.CostEstimate(flops=flops, bytes_accessed=moved, transcendentals=0),
    )(*ins)


def swaps(count):
    near = [(i, i ^ 1) for i in range(count)]
    far = [pair for i in range(1, count - 1, 2) for pair in ((i, i + 1), (i + 1, i))]
    return near, far


def local(state, sources, weight_index):
    img_count, slab_count = lax.axis_size("img"), lax.axis_size("slab")
    img_rank, slab_rank = lax.axis_index("img"), lax.axis_index("slab")
    per_dev, _, depth, _, _ = state.shape
    images, total = per_dev * img_count, depth * slab_count
    even_img, even_slab = img_rank % 2 == 0, slab_rank % 2 == 0

    top = state[:, :, -HALO:].transpose(1, 2, 3, 0, 4)
    bottom = state[:, :, :HALO].transpose(1, 2, 3, 0, 4)
    body = lax.optimization_barrier(state).transpose(1, 2, 3, 0, 4)
    near, far = swaps(slab_count)
    side_a = lax.ppermute(jnp.where(even_slab, top, bottom), "slab", near)
    side_b = lax.ppermute(jnp.where(even_slab, bottom, top), "slab", far)

    low = jnp.where(even_slab, side_b, side_a)[:, 2:]
    high = jnp.where(even_slab, side_a, side_b)[:, :2]
    ends = [
        jnp.concatenate([low[:, :, :, i], body[:, :, :, i], high[:, :, :, i]], axis=1).reshape(-1, 128)
        for i in (0, per_dev - 1)
    ]
    near, far = swaps(img_count)
    image_a = lax.ppermute(jnp.where(even_img, ends[1], ends[0]), "img", near)
    image_b = lax.ppermute(jnp.where(even_img, ends[0], ends[1]), "img", far)
    before = jnp.where(even_img, image_b, image_a)
    after = jnp.where(even_img, image_a, image_b)

    place = jnp.stack(
        [
            slab_rank * depth,
            jnp.where(even_slab, depth + HALO, 0),
            jnp.where(even_slab, 0, depth + HALO),
            img_rank * per_dev,
        ]
    ).astype(jnp.int32)
    wide = jax.ShapeDtypeStruct((2, depth + 2 * HALO, GX, 8, 128), F32)
    tile = jax.ShapeDtypeStruct((8, 128), F32)
    ext, mu, half, own, squares = call(
        functools.partial(drift_kernel, total, depth),
        (place, body, side_a, side_b),
        [SMEM, ANY, ANY, ANY],
        [wide, wide, wide, wide, tile],
        [pltpu.SemaphoreType.DMA((3,))],
        flops=20_000_000,
        moved=8_000_000,
    )
    sums = call(
        functools.partial(sums_kernel, depth),
        (ext, before, after, squares),
        [VMEM] * 4,
        jax.ShapeDtypeStruct((slab_count, 128), F32),
    )
    sums = lax.all_to_all(sums, "slab", 0, 0, tiled=True)
    weight = jnp.broadcast_to(((weight_index.astype(F32) + 1.0) / (WLEVELS + 1.0))[:, None], (8, 128))
    rows = 4 * GX
    updated = call(
        functools.partial(update_kernel, total, depth, images),
        (place, ext, before, after, mu, half, own, sums, weight),
        [SMEM] + [VMEM] * 8,
        jax.ShapeDtypeStruct((depth // 2, (rows + 1) * 8, 128), F32),
        [pltpu.VMEM(wide.shape, F32)] * 3,
    )
    got = lax.all_to_all(updated, "img", 0, 0, tiled=True)
    starts = (sources // per_dev) * ((rows + 1) * 8) + (sources % per_dev) * rows
    new = call(
        functools.partial(mix_kernel, images, rows),
        (starts.T.reshape(-1), got.reshape(-1, 128)),
        [SMEM, VMEM],
        jax.ShapeDtypeStruct((images * rows, 128), F32),
    )
    new = lax.all_to_all(new.reshape(img_count, per_dev, 2, 2, GX, 128), "img", 0, 0, tiled=True)
    return new.transpose(1, 2, 0, 3, 4, 5).reshape(state.shape)


def solution(mesh):
    return jax.shard_map(
        local,
        mesh=mesh,
        in_specs=(P("img", None, "slab", None, None), P(), P("img")),
        out_specs=P("img", None, "slab", None, None),
        check_vma=False,
    )
```

```python
import functools

import jax
import jax.numpy as jnp
from jax import lax
from jax.experimental import pallas as pl
from jax.experimental.pallas import tpu as pltpu
from jax.sharding import PartitionSpec as P

WLEVELS = 16
KAPPA = 0.25
COUPLE = 0.3
STEP_SIZE = 0.004
EPSILON = 1e-06

F32 = jnp.float32
GX = 4
LIMIT = 14 * 1024 * 1024
MOST = 121 * 512 * 1024
UNROLL = 2


def turn(value, shift):
    return pltpu.roll(value, shift % 128, 1)


def recip(d):
    r = pltpu.reciprocal(d, approx=True)
    r = r * (2.0 - d * r)
    return r * (2.0 - d * r)


def load(ref, z):
    return [[ref[f, z, x] for x in range(GX)] for f in range(2)]


def store(ref, z, layer):
    for f in range(2):
        for x in range(GX):
            ref[f, z, x] = layer[f][x]


def each(fn, *layers):
    return [[fn(*(layer[f][x] for layer in layers)) for x in range(GX)] for f in range(2)]


def potential(below, here, above):
    mu, half = [], []
    for f in range(2):
        mu.append([])
        half.append([])
        for x in range(GX):
            phi = here[f][x]
            around = below[f][x] + above[f][x]
            around = around + (here[f][(x + 1) % GX] + here[f][(x - 1) % GX])
            around = around + (turn(phi, 1) + turn(phi, -1))
            square = phi * phi
            mu[f].append(phi * (square + (6.0 * KAPPA - 1.0)) + COUPLE * here[1 - f][x] - KAPPA * around)
            half[f].append(0.25 + 0.5 * recip(1.0 + square))
    return mu, half


def face(mu, half, mu_up, half_up):
    return each(lambda p, h, q, k: (h + k) * (q - p), mu, half, mu_up, half_up)


def outflow(mu, half, lower, upper):
    layer = []
    for f in range(2):
        p, h = mu[f], half[f]
        side = [(h[x] + h[(x + 1) % GX]) * (p[(x + 1) % GX] - p[x]) for x in range(GX)]
        along = [(h[x] + turn(h[x], -1)) * (turn(p[x], -1) - p[x]) for x in range(GX)]
        layer.append(
            [
                (side[x] - side[x - 1]) + (along[x] - turn(along[x], 1)) + (upper[f][x] - lower[f][x])
                for x in range(GX)
            ]
        )
    return layer


def drift_kernel(depth, body, fields):
    mu, half, own, kept = (fields.at[i] for i in range(4))
    for z in (0, depth - 1):
        store(kept, z, load(body, z))

    def first_fields(z, carry):
        here = load(body, z)
        store(kept, z, here)
        p, h = potential(load(body, z - 1), here, load(body, z + 1))
        store(mu, z, p)
        store(half, z, h)
        return carry

    lax.fori_loop(1, depth - 1, first_fields, 0, unroll=2)

    def flux(z, lower):
        p, h = load(mu, z), load(half, z)
        upper = face(p, h, load(mu, z + 1), load(half, z + 1))
        store(own, z, outflow(p, h, lower, upper))
        return upper

    first = face(load(mu, 1), load(half, 1), load(mu, 2), load(half, 2))
    lax.fori_loop(2, depth - 2, flux, first, unroll=4)


def rim(depth, phi, known, low_open, high_open, reach):
    fields = {}
    for z in [*range(-reach, 1), *range(depth - 1, depth + reach)]:
        fields[z] = potential(phi(z - 1), phi(z), phi(z + 1))
    for z in (1, 2, depth - 3, depth - 2):
        fields[z] = known(z)
    faces, drifts = {}, {}
    for z in [*range(-reach, 2), *range(depth - 3, depth + reach - 1)]:
        faces[z] = face(*fields[z], *fields[z + 1])
    faces[-1] = each(lambda v: v * low_open, faces[-1])
    faces[depth - 1] = each(lambda v: v * high_open, faces[depth - 1])
    for z in [*range(1 - reach, 2), *range(depth - 2, depth + reach - 1)]:
        drifts[z] = outflow(*fields[z], faces[z - 1], faces[z])
    return fields, drifts


def ends_open():
    rank = lax.axis_index("slab")
    low = jnp.where(rank > 0, 1.0, 0.0).astype(F32)
    high = jnp.where(rank < lax.axis_size("slab") - 1, 1.0, 0.0).astype(F32)
    return low, high


def even(axis):
    return 1 - lax.axis_index(axis) % 2


def neighbours(here, before, after, f, z, x, rows):
    index = (f * rows + (z + 2)) * GX + x
    sub = lax.broadcasted_iota(jnp.int32, (8, 128), 0)
    prev = jnp.where(sub == 0, before[pl.ds(index, 1), :], pltpu.roll(here, 1, 0))
    following = jnp.where(sub == 7, after[pl.ds(index, 1), :], pltpu.roll(here, 7, 0))
    return prev, following


def fetch(pairs, sems):
    copies = [pltpu.make_async_copy(source, target, sems.at[i]) for i, (source, target) in enumerate(pairs)]
    for copy in copies:
        copy.start()

    def wait():
        for copy in copies:
            copy.wait()

    return wait


def arrivals(side_a, side_b, image_a, image_b, side, image, sems):
    slab, img = even("slab"), even("img")
    return fetch(
        [
            (side_a, side.at[slab]),
            (side_b, side.at[1 - slab]),
            (image_a, image.at[img]),
            (image_b, image.at[1 - img]),
        ],
        sems,
    )


def layer_of(depth, body, side):
    def phi(z):
        return load(side.at[0], z + 4) if z < 0 else load(side.at[1], z - depth) if z >= depth else load(body, z)

    return phi


def sums_kernel(depth, side_a, side_b, image_a, image_b, fields, sums, side, image, sems):
    arrived = arrivals(side_a, side_b, image_a, image_b, side, image, sems)
    mu, half, own, body = (fields.at[i] for i in range(4))

    def squares(z, kept):
        one, two = jnp.zeros((8, 128), F32), jnp.zeros((8, 128), F32)
        for x in range(GX):
            one = one + own[0, z, x] * own[0, z, x]
            two = two + own[1, z, x] * own[1, z, x]
        return kept + (one + two)

    kept = lax.fori_loop(2, depth - 2, squares, jnp.zeros((8, 128), F32), unroll=4)
    arrived()
    _, drifts = rim(depth, layer_of(depth, body, side), lambda z: (load(mu, z), load(half, z)), *ends_open(), 1)
    for z in (0, 1, depth - 2, depth - 1):
        for f in range(2):
            for x in range(GX):
                kept = kept + drifts[z][f][x] * drifts[z][f][x]

    def step(z, acc):
        for f in range(2):
            for x in range(GX):
                prev, following = neighbours(body[f, z, x], image.at[0], image.at[1], f, z, x, depth + 4)
                d = following - prev
                acc = acc + d * d
        return acc

    acc = lax.fori_loop(0, depth, step, jnp.zeros((8, 128), F32), unroll=4)
    sub = lax.broadcasted_iota(jnp.int32, (8, 128), 0)
    lane = lax.broadcasted_iota(jnp.int32, (8, 128), 1)
    drift_sq = jnp.sum(kept, axis=1, keepdims=True)
    tangent_sq = jnp.sum(acc, axis=1, keepdims=True)
    row = jnp.where(lane == sub, drift_sq, jnp.where(lane == sub + 8, tangent_sq, 0.0))
    sums[...] = jnp.broadcast_to(jnp.sum(row, axis=0, keepdims=True), sums.shape)


def rim_layers(depth):
    fields = (-2, -1, 0, depth - 1, depth, depth + 1)
    drifts = (-2, -1, 0, 1, depth - 2, depth - 1, depth, depth + 1)
    return {z: i for i, z in enumerate(fields)}, {z: i for i, z in enumerate(drifts)}


def prepare_kernel(depth, side_a, side_b, image_a, image_b, fields, diff, both, rim_mu, rim_half, rim_own, *scratch):
    side, image, sems, body, ends, more = scratch
    arrived = arrivals(side_a, side_b, image_a, image_b, side, image, sems)
    pairs = [(fields.at[3], body)]
    for i in range(2):
        pairs.append((fields.at[i, :, pl.ds(1, 2)], ends.at[i, :, pl.ds(0, 2)]))
        pairs.append((fields.at[i, :, pl.ds(depth - 3, 2)], ends.at[i, :, pl.ds(2, 2)]))
    fetch(pairs, more)()
    arrived()
    place = {1: 0, 2: 1, depth - 3: 2, depth - 2: 3}
    phi = layer_of(depth, body, side)
    known, drifts = rim(depth, phi, lambda z: (load(ends.at[0], place[z]), load(ends.at[1], place[z])), *ends_open(), 3)
    slot, drift_slot = rim_layers(depth)
    for z, i in slot.items():
        store(rim_mu, i, known[z][0])
        store(rim_half, i, known[z][1])
    for z, i in drift_slot.items():
        store(rim_own, i, drifts[z])

    def images(z, here):
        for f in range(2):
            for x in range(GX):
                prev, following = neighbours(here[f][x], image.at[0], image.at[1], f, z, x, depth + 4)
                diff[f, z + 2, x] = following - prev
                both[f, z + 2, x] = following + prev

    for z in (-2, -1, depth, depth + 1):
        images(z, phi(z))

    def inside(z, carry):
        images(z, load(body, z))
        return carry

    lax.fori_loop(0, depth, inside, 0, unroll=4)


def update_kernel(depth, images, given, diff_given, both_given, rim_mu_given, rim_half_given, rim_own_given, *refs):
    sums, level, out, m_ref, bar, inner, fields, diff, both, rim_mu, rim_half, rim_own, sems = refs
    cut = depth // 4
    parts = [(2, cut), (cut, depth - 2)]
    rim_here = fetch(
        [
            (rim_own_given, rim_own),
            (diff_given.at[:, pl.ds(0, 4)], diff.at[:, pl.ds(0, 4)]),
            (diff_given.at[:, pl.ds(depth, 4)], diff.at[:, pl.ds(depth, 4)]),
        ],
        sems.at[0],
    )
    parts_here = []
    for i, (low, high) in enumerate(parts):
        own_part, diff_part = pl.ds(low, high - low), pl.ds(low + 2, high - low)
        parts_here.append(
            fetch(
                [
                    (given.at[2, :, own_part], fields.at[2, :, own_part]),
                    (diff_given.at[:, diff_part], diff.at[:, diff_part]),
                ],
                sems.at[1 + i],
            )
        )
    flux_here = fetch(
        [
            (rim_mu_given, rim_mu),
            (rim_half_given, rim_half),
            (given.at[0], fields.at[0]),
            (given.at[1], fields.at[1]),
        ],
        sems.at[3],
    )
    rest_here = fetch([(given.at[3], fields.at[3]), (both_given, both)], sems.at[4])
    mu, half, own, body = (fields.at[i] for i in range(4))
    slot, drift_slot = rim_layers(depth)
    sub = lax.broadcasted_iota(jnp.int32, (8, 128), 0)
    lane = lax.broadcasted_iota(jnp.int32, (8, 128), 1)
    added = jnp.sum(sums[...], axis=0, keepdims=True)
    drift_sq = jnp.sum(jnp.where(lane == sub, added, 0.0), axis=1, keepdims=True)
    tangent_sq = jnp.sum(jnp.where(lane == sub + 8, added, 0.0), axis=1, keepdims=True)
    rate = (images - 1) / 2.0
    scale = jnp.sqrt(drift_sq) / jnp.sqrt(tangent_sq * (rate * rate) + EPSILON)
    by_tangent = jnp.broadcast_to(scale * rate, (8, 128))
    by_second = jnp.broadcast_to(scale * scale * float((images - 1) ** 2), (8, 128))
    index = lax.axis_index("img") * 8 + sub
    step_size = jnp.where((index > 0) & (index < images - 1), STEP_SIZE, 0.0).astype(F32)
    low_open, high_open = ends_open()
    weight = jnp.zeros((8, 128), F32)
    for i in range(8):
        weight = jnp.where(sub == i, level[i].astype(F32), weight)
    weight = (weight + 1.0) / (WLEVELS + 1.0)

    def momentum(z, drift):
        store(m_ref, z + 2, each(lambda d, b: by_tangent * d - b, load(diff, z + 2), drift))

    rim_here()
    for z, i in drift_slot.items():
        momentum(z, load(rim_own, i))

    def inside(z, carry):
        momentum(z, load(own, z))
        return carry

    for (first, last), here in zip(parts, parts_here):
        here()
        lax.fori_loop(first, last, inside, 0, unroll=2)
    flux_here()

    def known(z):
        if isinstance(z, int) and z in slot:
            return load(rim_mu, slot[z]), load(rim_half, slot[z])
        return load(mu, z), load(half, z)

    def pair(z, up):
        (p, h), (q, k) = known(z), known(up)
        m, n = load(m_ref, z + 2), load(m_ref, up + 2)
        g = each(lambda a, b, c, d: (a + b) * (d - c), h, k, m, n)
        return g, each(lambda a, b, c, d: (b - a) * (d - c), p, q, m, n)

    def adjoint(z, lower, upper, is_open=None):
        p, h = known(z)
        m = load(m_ref, z + 2)
        for f in range(2):
            side = []
            for x in range(GX):
                n = (x + 1) % GX
                dm = m[f][n] - m[f][x]
                side.append(((h[f][x] + h[f][n]) * dm, dm * (p[f][n] - p[f][x])))
            for x in range(GX):
                dm = turn(m[f][x], -1) - m[f][x]
                g_y = (h[f][x] + turn(h[f][x], -1)) * dm
                q_y = dm * (turn(p[f][x], -1) - p[f][x])
                g = (side[x][0] - side[x - 1][0]) + (g_y - turn(g_y, 1)) + (upper[0][f][x] - lower[0][f][x])
                q = (side[x][1] + side[x - 1][1]) + (q_y + turn(q_y, 1)) + (upper[1][f][x] + lower[1][f][x])
                bar[f, z + 1, x] = g if is_open is None else g * is_open
                inner[f, z + 1, x] = q

    def shut(faces, is_open):
        return tuple(each(lambda v: v * is_open, layer) for layer in faces)

    faces = pair(-2, -1)
    upper = shut(pair(-1, 0), low_open)
    adjoint(-1, faces, upper, low_open)
    faces, upper = upper, pair(0, 1)
    adjoint(0, faces, upper)

    def within(z, lower):
        upper = pair(z, z + 1)
        adjoint(z, lower, upper)
        return upper

    faces = lax.fori_loop(1, depth - 2, within, upper, unroll=2)
    upper = pair(depth - 2, depth - 1)
    adjoint(depth - 2, faces, upper)
    faces, upper = upper, shut(pair(depth - 1, depth), high_open)
    adjoint(depth - 1, faces, upper)
    adjoint(depth, upper, pair(depth, depth + 1), high_open)

    def finish(r, carry):
        for zz in range(2):
            z = 2 * r + zz
            _, h = known(z)
            for f in range(2):
                g = [bar[f, z + 1, x] for x in range(GX)]
                for x in range(GX):
                    phi = body[f, z, x]
                    around = bar[f, z, x] + bar[f, z + 2, x]
                    around = around + (g[(x + 1) % GX] + g[(x - 1) % GX])
                    around = around + (turn(g[x], 1) + turn(g[x], -1))
                    inverse = 2.0 * h[f][x] - 0.5
                    pulled = phi * (inverse * inverse) * inner[f, z + 1, x]
                    pulled = pulled + (3.0 * (phi * phi) + (6.0 * KAPPA - 1.0)) * g[x]
                    pulled = pulled + COUPLE * bar[1 - f, z + 1, x] - KAPPA * around
                    second = both[f, z + 2, x] - 2.0 * phi
                    new = phi + step_size * (by_second * second + pulled)
                    out[r, pl.ds((f * 2 + zz) * GX + x, 8, stride=4 * GX), :] = new
        out[r, pl.ds(32 * GX, 8), :] = weight
        return carry

    rest_here()
    finish(0, 0)
    lax.fori_loop(1, depth // 2 - 1, finish, 0, unroll=UNROLL)
    finish(depth // 2 - 1, 0)


def mix_kernel(images, rows, starts, got, out):
    block = (rows + 1) * 8

    def step(j, carry):
        a = pl.multiple_of(starts[j], 8)
        b = pl.multiple_of(starts[images + j], 8)
        w = got[pl.ds((j // 8) * block + rows * 8 + j % 8, 1), :]
        for part in range(0, rows, 8):
            one, two = got[pl.ds(a + part, 8), :], got[pl.ds(b + part, 8), :]
            out[pl.ds(pl.multiple_of(j * rows + part, 8), 8), :] = w * one + (1.0 - w) * two
        return carry

    lax.fori_loop(0, images, step, 0, unroll=8)


ANY = pl.BlockSpec(memory_space=pl.ANY)
VMEM = pl.BlockSpec(memory_space=pltpu.VMEM)
SMEM = pl.BlockSpec(memory_space=pltpu.SMEM)


def call(kernel, ins, in_specs, outs, scratch=(), flops=0, moved=0, limit=LIMIT):
    return pl.pallas_call(
        kernel,
        in_specs=in_specs,
        out_specs=jax.tree.map(lambda _: VMEM, outs),
        out_shape=outs,
        scratch_shapes=list(scratch),
        compiler_params=pltpu.CompilerParams(vmem_limit_bytes=limit),
        cost_estimate=pl.CostEstimate(flops=flops, bytes_accessed=moved, transcendentals=0),
    )(*ins)


def swaps(count):
    near = [(i, i ^ 1) for i in range(count)]
    far = [pair for i in range(1, count - 1, 2) for pair in ((i, i + 1), (i + 1, i))]
    return near, far


def local(state, sources, weight_index):
    img_count, slab_count = lax.axis_size("img"), lax.axis_size("slab")
    img_rank, slab_rank = lax.axis_index("img"), lax.axis_index("slab")
    per_dev, _, depth, _, _ = state.shape
    images = per_dev * img_count
    even_img, even_slab = img_rank % 2 == 0, slab_rank % 2 == 0

    near, far = swaps(slab_count)

    top = state[:, :, depth - 4 :].transpose(1, 2, 3, 0, 4)
    bottom = state[:, :, :4].transpose(1, 2, 3, 0, 4)
    side_a = lax.ppermute(jnp.where(even_slab, top, bottom), "slab", near)
    side_b = lax.ppermute(jnp.where(even_slab, bottom, top), "slab", far)
    body = lax.optimization_barrier(state).transpose(1, 2, 3, 0, 4)
    fields = call(
        functools.partial(drift_kernel, depth),
        (body,),
        [VMEM],
        jax.ShapeDtypeStruct((4, *body.shape), F32),
        flops=16_000_000,
        moved=4_000_000,
    )

    low, high = jnp.where(even_slab, side_b, side_a)[:, 2:], jnp.where(even_slab, side_a, side_b)[:, :2]
    ends = [
        jnp.concatenate([low[:, :, :, i], state[i], high[:, :, :, i]], axis=1).reshape(-1, 128)
        for i in (0, per_dev - 1)
    ]
    near, far = swaps(img_count)
    image_a = lax.ppermute(jnp.where(even_img, ends[1], ends[0]), "img", near)
    image_b = lax.ppermute(jnp.where(even_img, ends[0], ends[1]), "img", far)

    def layers(count):
        return (2, count, GX, 8, 128)

    brought = [
        pltpu.VMEM((2, *layers(4)), F32),
        pltpu.VMEM((2, *image_a.shape), F32),
        pltpu.SemaphoreType.DMA((4,)),
    ]
    around = (side_a, side_b, image_a, image_b, fields)
    sums = call(
        functools.partial(sums_kernel, depth),
        around,
        [ANY] * 4 + [VMEM],
        jax.ShapeDtypeStruct((slab_count, 128), F32),
        brought,
    )
    sums = lax.all_to_all(sums, "slab", 0, 0, tiled=True)
    wide = layers(depth + 4)
    prepared = call(
        functools.partial(prepare_kernel, depth),
        around,
        [ANY] * 5,
        [jax.ShapeDtypeStruct(shape, F32) for shape in (wide, wide, layers(6), layers(6), layers(8))],
        brought
        + [pltpu.VMEM(layers(depth), F32), pltpu.VMEM((2, *layers(4)), F32), pltpu.SemaphoreType.DMA((5,))],
        flops=8_000_000,
        moved=4_000_000,
        limit=MOST,
    )
    rows = 4 * GX
    updated = call(
        functools.partial(update_kernel, depth, images),
        (fields, *prepared, sums, weight_index),
        [ANY] * 6 + [VMEM, SMEM],
        jax.ShapeDtypeStruct((depth // 2, (rows + 1) * 8, 128), F32),
        [pltpu.VMEM(wide, F32)]
        + [pltpu.VMEM(layers(depth + 2), F32)] * 2
        + [pltpu.VMEM(array.shape, F32) for array in (fields, *prepared)]
        + [pltpu.SemaphoreType.DMA((5, 4))],
        limit=MOST,
    )
    got = lax.all_to_all(updated, "img", 0, 0, tiled=True)
    starts = (sources // per_dev) * ((rows + 1) * 8) + (sources % per_dev) * rows
    new = call(
        functools.partial(mix_kernel, images, rows),
        (starts.T.reshape(-1), got.reshape(-1, 128)),
        [SMEM, VMEM],
        jax.ShapeDtypeStruct((images * rows, 128), F32),
    )
    new = lax.all_to_all(new.reshape(img_count, per_dev, 2, 2, GX, 128), "img", 0, 0, tiled=True)
    return new.transpose(1, 2, 0, 3, 4, 5).reshape(state.shape)


def solution(mesh):
    return jax.shard_map(
        local,
        mesh=mesh,
        in_specs=(P("img", None, "slab", None, None), P(), P("img")),
        out_specs=P("img", None, "slab", None, None),
        check_vma=False,
    )
```

```python
import functools

import jax
import jax.numpy as jnp
from jax import lax
from jax.experimental import pallas as pl
from jax.experimental.pallas import tpu as pltpu
from jax.sharding import PartitionSpec as P

WLEVELS = 16
KAPPA = 0.25
COUPLE = 0.3
STEP_SIZE = 0.004
EPSILON = 1e-06

F32 = jnp.float32
GX = 4
LIMIT = 14 * 1024 * 1024
MOST = 121 * 512 * 1024
UNROLL = 2


def turn(value, shift):
    return pltpu.roll(value, shift % 128, 1)


def recip(d):
    r = pltpu.reciprocal(d, approx=True)
    r = r * (2.0 - d * r)
    return r * (2.0 - d * r)


def load(ref, z):
    return [[ref[f, z, x] for x in range(GX)] for f in range(2)]


def store(ref, z, layer):
    for f in range(2):
        for x in range(GX):
            ref[f, z, x] = layer[f][x]


def each(fn, *layers):
    return [[fn(*(layer[f][x] for layer in layers)) for x in range(GX)] for f in range(2)]


def potential(below, here, above):
    mu, half = [], []
    for f in range(2):
        mu.append([])
        half.append([])
        for x in range(GX):
            phi = here[f][x]
            around = below[f][x] + above[f][x]
            around = around + (here[f][(x + 1) % GX] + here[f][(x - 1) % GX])
            around = around + (turn(phi, 1) + turn(phi, -1))
            square = phi * phi
            mu[f].append(phi * (square + (6.0 * KAPPA - 1.0)) + COUPLE * here[1 - f][x] - KAPPA * around)
            half[f].append(0.25 + 0.5 * recip(1.0 + square))
    return mu, half


def face(mu, half, mu_up, half_up):
    return each(lambda p, h, q, k: (h + k) * (q - p), mu, half, mu_up, half_up)


def outflow(mu, half, lower, upper):
    layer = []
    for f in range(2):
        p, h = mu[f], half[f]
        side = [(h[x] + h[(x + 1) % GX]) * (p[(x + 1) % GX] - p[x]) for x in range(GX)]
        along = [(h[x] + turn(h[x], -1)) * (turn(p[x], -1) - p[x]) for x in range(GX)]
        layer.append(
            [
                (side[x] - side[x - 1]) + (along[x] - turn(along[x], 1)) + (upper[f][x] - lower[f][x])
                for x in range(GX)
            ]
        )
    return layer


def drift_kernel(depth, body, fields):
    mu, half, own, kept = (fields.at[i] for i in range(4))
    for z in (0, depth - 1):
        store(kept, z, load(body, z))

    def first_fields(z, carry):
        here = load(body, z)
        store(kept, z, here)
        p, h = potential(load(body, z - 1), here, load(body, z + 1))
        store(mu, z, p)
        store(half, z, h)
        return carry

    lax.fori_loop(1, depth - 1, first_fields, 0, unroll=2)

    def flux(z, lower):
        p, h = load(mu, z), load(half, z)
        upper = face(p, h, load(mu, z + 1), load(half, z + 1))
        store(own, z, outflow(p, h, lower, upper))
        return upper

    first = face(load(mu, 1), load(half, 1), load(mu, 2), load(half, 2))
    lax.fori_loop(2, depth - 2, flux, first, unroll=4)


def rim(depth, phi, known, low_open, high_open, reach):
    fields = {}
    for z in [*range(-reach, 1), *range(depth - 1, depth + reach)]:
        fields[z] = potential(phi(z - 1), phi(z), phi(z + 1))
    for z in (1, 2, depth - 3, depth - 2):
        fields[z] = known(z)
    faces, drifts = {}, {}
    for z in [*range(-reach, 2), *range(depth - 3, depth + reach - 1)]:
        faces[z] = face(*fields[z], *fields[z + 1])
    faces[-1] = each(lambda v: v * low_open, faces[-1])
    faces[depth - 1] = each(lambda v: v * high_open, faces[depth - 1])
    for z in [*range(1 - reach, 2), *range(depth - 2, depth + reach - 1)]:
        drifts[z] = outflow(*fields[z], faces[z - 1], faces[z])
    return fields, drifts


def ends_open():
    rank = lax.axis_index("slab")
    low = jnp.where(rank > 0, 1.0, 0.0).astype(F32)
    high = jnp.where(rank < lax.axis_size("slab") - 1, 1.0, 0.0).astype(F32)
    return low, high


def even(axis):
    return 1 - lax.axis_index(axis) % 2


def neighbours(here, before, after, f, z, x, rows):
    index = (f * rows + (z + 2)) * GX + x
    sub = lax.broadcasted_iota(jnp.int32, (8, 128), 0)
    prev = jnp.where(sub == 0, before[pl.ds(index, 1), :], pltpu.roll(here, 1, 0))
    following = jnp.where(sub == 7, after[pl.ds(index, 1), :], pltpu.roll(here, 7, 0))
    return prev, following


def fetch(pairs, sems):
    copies = [pltpu.make_async_copy(source, target, sems.at[i]) for i, (source, target) in enumerate(pairs)]
    for copy in copies:
        copy.start()

    def wait():
        for copy in copies:
            copy.wait()

    return wait


def arrivals(side_a, side_b, image_a, image_b, side, image, sems):
    slab, img = even("slab"), even("img")
    return fetch(
        [
            (side_a, side.at[slab]),
            (side_b, side.at[1 - slab]),
            (image_a, image.at[img]),
            (image_b, image.at[1 - img]),
        ],
        sems,
    )


def layer_of(depth, body, side):
    low_open, high_open = ends_open()

    def phi(z):
        if z < 0:
            return each(lambda v: jnp.where(low_open > 0.0, v, 0.0), load(side.at[0], z + 4))
        if z >= depth:
            return each(lambda v: jnp.where(high_open > 0.0, v, 0.0), load(side.at[1], z - depth))
        return load(body, z)

    return phi


def sums_kernel(depth, side_a, side_b, image_a, image_b, fields, sums, side, image, sems):
    arrived = arrivals(side_a, side_b, image_a, image_b, side, image, sems)
    mu, half, own, body = (fields.at[i] for i in range(4))

    def squares(z, kept):
        one, two = jnp.zeros((8, 128), F32), jnp.zeros((8, 128), F32)
        for x in range(GX):
            one = one + own[0, z, x] * own[0, z, x]
            two = two + own[1, z, x] * own[1, z, x]
        return kept + (one + two)

    kept = lax.fori_loop(2, depth - 2, squares, jnp.zeros((8, 128), F32), unroll=4)
    arrived()
    _, drifts = rim(depth, layer_of(depth, body, side), lambda z: (load(mu, z), load(half, z)), *ends_open(), 1)
    for z in (0, 1, depth - 2, depth - 1):
        for f in range(2):
            for x in range(GX):
                kept = kept + drifts[z][f][x] * drifts[z][f][x]

    def step(z, acc):
        for f in range(2):
            for x in range(GX):
                prev, following = neighbours(body[f, z, x], image.at[0], image.at[1], f, z, x, depth + 4)
                d = following - prev
                acc = acc + d * d
        return acc

    acc = lax.fori_loop(0, depth, step, jnp.zeros((8, 128), F32), unroll=4)
    sub = lax.broadcasted_iota(jnp.int32, (8, 128), 0)
    lane = lax.broadcasted_iota(jnp.int32, (8, 128), 1)
    drift_sq = jnp.sum(kept, axis=1, keepdims=True)
    tangent_sq = jnp.sum(acc, axis=1, keepdims=True)
    row = jnp.where(lane == sub, drift_sq, jnp.where(lane == sub + 8, tangent_sq, 0.0))
    sums[...] = jnp.broadcast_to(jnp.sum(row, axis=0, keepdims=True), sums.shape)


def rim_layers(depth):
    fields = (-2, -1, 0, depth - 1, depth, depth + 1)
    drifts = (-2, -1, 0, 1, depth - 2, depth - 1, depth, depth + 1)
    return {z: i for i, z in enumerate(fields)}, {z: i for i, z in enumerate(drifts)}


def prepare_kernel(depth, side_a, side_b, image_a, image_b, fields, diff, both, rim_mu, rim_half, rim_own, *scratch):
    side, image, sems, body, ends, more = scratch
    arrived = arrivals(side_a, side_b, image_a, image_b, side, image, sems)
    pairs = [(fields.at[3], body)]
    for i in range(2):
        pairs.append((fields.at[i, :, pl.ds(1, 2)], ends.at[i, :, pl.ds(0, 2)]))
        pairs.append((fields.at[i, :, pl.ds(depth - 3, 2)], ends.at[i, :, pl.ds(2, 2)]))
    fetch(pairs, more)()
    arrived()
    place = {1: 0, 2: 1, depth - 3: 2, depth - 2: 3}
    phi = layer_of(depth, body, side)
    known, drifts = rim(depth, phi, lambda z: (load(ends.at[0], place[z]), load(ends.at[1], place[z])), *ends_open(), 3)
    slot, drift_slot = rim_layers(depth)
    for z, i in slot.items():
        store(rim_mu, i, known[z][0])
        store(rim_half, i, known[z][1])
    for z, i in drift_slot.items():
        store(rim_own, i, drifts[z])

    def images(z, here):
        for f in range(2):
            for x in range(GX):
                prev, following = neighbours(here[f][x], image.at[0], image.at[1], f, z, x, depth + 4)
                diff[f, z + 2, x] = following - prev
                both[f, z + 2, x] = following + prev

    for z in (-2, -1, depth, depth + 1):
        images(z, phi(z))

    def inside(z, carry):
        images(z, load(body, z))
        return carry

    lax.fori_loop(0, depth, inside, 0, unroll=4)


def update_kernel(depth, images, given, diff_given, both_given, rim_mu_given, rim_half_given, rim_own_given, *refs):
    sums_given, level, out, m_ref, bar, inner, fields, diff, both, rim_mu, rim_half, rim_own, sums, sems = refs
    sums_here = fetch([(sums_given, sums)], sems.at[5])
    cut = depth // 4
    parts = [(2, cut), (cut, depth - 2)]
    rim_here = fetch(
        [
            (rim_own_given, rim_own),
            (diff_given.at[:, pl.ds(0, 4)], diff.at[:, pl.ds(0, 4)]),
            (diff_given.at[:, pl.ds(depth, 4)], diff.at[:, pl.ds(depth, 4)]),
        ],
        sems.at[0],
    )
    parts_here = []
    for i, (low, high) in enumerate(parts):
        own_part, diff_part = pl.ds(low, high - low), pl.ds(low + 2, high - low)
        parts_here.append(
            fetch(
                [
                    (given.at[2, :, own_part], fields.at[2, :, own_part]),
                    (diff_given.at[:, diff_part], diff.at[:, diff_part]),
                ],
                sems.at[1 + i],
            )
        )
    flux_here = fetch(
        [
            (rim_mu_given, rim_mu),
            (rim_half_given, rim_half),
            (given.at[0], fields.at[0]),
            (given.at[1], fields.at[1]),
        ],
        sems.at[3],
    )
    rest_here = fetch([(given.at[3], fields.at[3]), (both_given, both)], sems.at[4])
    mu, half, own, body = (fields.at[i] for i in range(4))
    slot, drift_slot = rim_layers(depth)
    sub = lax.broadcasted_iota(jnp.int32, (8, 128), 0)
    lane = lax.broadcasted_iota(jnp.int32, (8, 128), 1)
    sums_here()
    added = jnp.sum(sums[...], axis=0, keepdims=True)
    drift_sq = jnp.sum(jnp.where(lane == sub, added, 0.0), axis=1, keepdims=True)
    tangent_sq = jnp.sum(jnp.where(lane == sub + 8, added, 0.0), axis=1, keepdims=True)
    rate = (images - 1) / 2.0
    scale = jnp.sqrt(drift_sq) / jnp.sqrt(tangent_sq * (rate * rate) + EPSILON)
    by_tangent = jnp.broadcast_to(scale * rate, (8, 128))
    by_second = jnp.broadcast_to(scale * scale * float((images - 1) ** 2), (8, 128))
    index = lax.axis_index("img") * 8 + sub
    step_size = jnp.where((index > 0) & (index < images - 1), STEP_SIZE, 0.0).astype(F32)
    low_open, high_open = ends_open()
    weight = jnp.zeros((8, 128), F32)
    for i in range(8):
        weight = jnp.where(sub == i, level[i].astype(F32), weight)
    weight = (weight + 1.0) / (WLEVELS + 1.0)

    def momentum(z, drift):
        store(m_ref, z + 2, each(lambda d, b: by_tangent * d - b, load(diff, z + 2), drift))

    rim_here()
    for z, i in drift_slot.items():
        momentum(z, load(rim_own, i))

    def inside(z, carry):
        momentum(z, load(own, z))
        return carry

    for (first, last), here in zip(parts, parts_here):
        here()
        lax.fori_loop(first, last, inside, 0, unroll=2)
    flux_here()

    def known(z):
        if isinstance(z, int) and z in slot:
            return load(rim_mu, slot[z]), load(rim_half, slot[z])
        return load(mu, z), load(half, z)

    def pair(z, up):
        (p, h), (q, k) = known(z), known(up)
        m, n = load(m_ref, z + 2), load(m_ref, up + 2)
        g = each(lambda a, b, c, d: (a + b) * (d - c), h, k, m, n)
        return g, each(lambda a, b, c, d: (b - a) * (d - c), p, q, m, n)

    def adjoint(z, lower, upper, is_open=None):
        p, h = known(z)
        m = load(m_ref, z + 2)
        for f in range(2):
            side = []
            for x in range(GX):
                n = (x + 1) % GX
                dm = m[f][n] - m[f][x]
                side.append(((h[f][x] + h[f][n]) * dm, dm * (p[f][n] - p[f][x])))
            for x in range(GX):
                dm = turn(m[f][x], -1) - m[f][x]
                g_y = (h[f][x] + turn(h[f][x], -1)) * dm
                q_y = dm * (turn(p[f][x], -1) - p[f][x])
                g = (side[x][0] - side[x - 1][0]) + (g_y - turn(g_y, 1)) + (upper[0][f][x] - lower[0][f][x])
                q = (side[x][1] + side[x - 1][1]) + (q_y + turn(q_y, 1)) + (upper[1][f][x] + lower[1][f][x])
                bar[f, z + 1, x] = g if is_open is None else g * is_open
                inner[f, z + 1, x] = q

    def shut(faces, is_open):
        return tuple(each(lambda v: v * is_open, layer) for layer in faces)

    faces = pair(-2, -1)
    upper = shut(pair(-1, 0), low_open)
    adjoint(-1, faces, upper, low_open)
    faces, upper = upper, pair(0, 1)
    adjoint(0, faces, upper)

    def within(z, lower):
        upper = pair(z, z + 1)
        adjoint(z, lower, upper)
        return upper

    faces = lax.fori_loop(1, depth - 2, within, upper, unroll=2)
    upper = pair(depth - 2, depth - 1)
    adjoint(depth - 2, faces, upper)
    faces, upper = upper, shut(pair(depth - 1, depth), high_open)
    adjoint(depth - 1, faces, upper)
    adjoint(depth, upper, pair(depth, depth + 1), high_open)

    def finish(r, carry):
        for zz in range(2):
            z = 2 * r + zz
            _, h = known(z)
            for f in range(2):
                g = [bar[f, z + 1, x] for x in range(GX)]
                for x in range(GX):
                    phi = body[f, z, x]
                    around = bar[f, z, x] + bar[f, z + 2, x]
                    around = around + (g[(x + 1) % GX] + g[(x - 1) % GX])
                    around = around + (turn(g[x], 1) + turn(g[x], -1))
                    inverse = 2.0 * h[f][x] - 0.5
                    pulled = phi * (inverse * inverse) * inner[f, z + 1, x]
                    pulled = pulled + (3.0 * (phi * phi) + (6.0 * KAPPA - 1.0)) * g[x]
                    pulled = pulled + COUPLE * bar[1 - f, z + 1, x] - KAPPA * around
                    second = both[f, z + 2, x] - 2.0 * phi
                    new = phi + step_size * (by_second * second + pulled)
                    out[r, pl.ds((f * 2 + zz) * GX + x, 8, stride=4 * GX), :] = new
        out[r, pl.ds(32 * GX, 8), :] = weight
        return carry

    rest_here()
    finish(0, 0)
    lax.fori_loop(1, depth // 2 - 1, finish, 0, unroll=UNROLL)
    finish(depth // 2 - 1, 0)


def mix_kernel(images, rows, starts, got, out):
    block = (rows + 1) * 8

    def step(j, carry):
        a = pl.multiple_of(starts[j], 8)
        b = pl.multiple_of(starts[images + j], 8)
        w = got[pl.ds((j // 8) * block + rows * 8 + j % 8, 1), :]
        for part in range(0, rows, 8):
            one, two = got[pl.ds(a + part, 8), :], got[pl.ds(b + part, 8), :]
            out[pl.ds(pl.multiple_of(j * rows + part, 8), 8), :] = w * one + (1.0 - w) * two
        return carry

    lax.fori_loop(0, images, step, 0, unroll=8)


ANY = pl.BlockSpec(memory_space=pl.ANY)
VMEM = pl.BlockSpec(memory_space=pltpu.VMEM)
SMEM = pl.BlockSpec(memory_space=pltpu.SMEM)


def call(kernel, ins, in_specs, outs, scratch=(), flops=0, moved=0, limit=LIMIT):
    return pl.pallas_call(
        kernel,
        in_specs=in_specs,
        out_specs=jax.tree.map(lambda _: VMEM, outs),
        out_shape=outs,
        scratch_shapes=list(scratch),
        compiler_params=pltpu.CompilerParams(vmem_limit_bytes=limit),
        cost_estimate=pl.CostEstimate(flops=flops, bytes_accessed=moved, transcendentals=0),
    )(*ins)


def swaps(count):
    near = [(i, i ^ 1) for i in range(count)]
    far = [pair for i in range(1, count, 2) for pair in ((i, (i + 1) % count), ((i + 1) % count, i))]
    return near, far


def local(state, sources, weight_index):
    img_count, slab_count = lax.axis_size("img"), lax.axis_size("slab")
    img_rank, slab_rank = lax.axis_index("img"), lax.axis_index("slab")
    per_dev, _, depth, _, _ = state.shape
    images = per_dev * img_count
    even_img, even_slab = img_rank % 2 == 0, slab_rank % 2 == 0

    near, far = swaps(slab_count)

    top = state[:, :, depth - 4 :].transpose(1, 2, 3, 0, 4)
    bottom = state[:, :, :4].transpose(1, 2, 3, 0, 4)
    side_a = lax.ppermute(jnp.where(even_slab, top, bottom), "slab", near)
    side_b = lax.ppermute(jnp.where(even_slab, bottom, top), "slab", far)
    body = lax.optimization_barrier(state).transpose(1, 2, 3, 0, 4)
    side_a, side_b, body = lax.optimization_barrier((side_a, side_b, body))
    fields = call(
        functools.partial(drift_kernel, depth),
        (body,),
        [VMEM],
        jax.ShapeDtypeStruct((4, *body.shape), F32),
        flops=16_000_000,
        moved=4_000_000,
    )

    low, high = jnp.where(even_slab, side_b, side_a)[:, 2:], jnp.where(even_slab, side_a, side_b)[:, :2]
    ends = [
        jnp.concatenate([low[:, :, :, i], state[i], high[:, :, :, i]], axis=1).reshape(-1, 128)
        for i in (0, per_dev - 1)
    ]
    near, far = swaps(img_count)
    image_a = lax.ppermute(jnp.where(even_img, ends[1], ends[0]), "img", near)
    image_b = lax.ppermute(jnp.where(even_img, ends[0], ends[1]), "img", far)

    def layers(count):
        return (2, count, GX, 8, 128)

    brought = [
        pltpu.VMEM((2, *layers(4)), F32),
        pltpu.VMEM((2, *image_a.shape), F32),
        pltpu.SemaphoreType.DMA((4,)),
    ]
    around = (side_a, side_b, image_a, image_b, fields)
    sums = call(
        functools.partial(sums_kernel, depth),
        around,
        [ANY] * 4 + [VMEM],
        jax.ShapeDtypeStruct((slab_count, 128), F32),
        brought,
    )
    sums = lax.all_to_all(sums, "slab", 0, 0, tiled=True)
    wide = layers(depth + 4)
    prepared = call(
        functools.partial(prepare_kernel, depth),
        around,
        [ANY] * 5,
        [jax.ShapeDtypeStruct(shape, F32) for shape in (wide, wide, layers(6), layers(6), layers(8))],
        brought
        + [pltpu.VMEM(layers(depth), F32), pltpu.VMEM((2, *layers(4)), F32), pltpu.SemaphoreType.DMA((5,))],
        flops=8_000_000,
        moved=4_000_000,
        limit=MOST,
    )
    rows = 4 * GX
    updated = call(
        functools.partial(update_kernel, depth, images),
        (fields, *prepared, sums, weight_index),
        [ANY] * 7 + [SMEM],
        jax.ShapeDtypeStruct((depth // 2, (rows + 1) * 8, 128), F32),
        [pltpu.VMEM(wide, F32)]
        + [pltpu.VMEM(layers(depth + 2), F32)] * 2
        + [pltpu.VMEM(array.shape, F32) for array in (fields, *prepared, sums)]
        + [pltpu.SemaphoreType.DMA((6, 4))],
        limit=MOST,
    )
    got = lax.all_to_all(updated, "img", 0, 0, tiled=True)
    starts = (sources // per_dev) * ((rows + 1) * 8) + (sources % per_dev) * rows
    new = call(
        functools.partial(mix_kernel, images, rows),
        (starts.T.reshape(-1), got.reshape(-1, 128)),
        [SMEM, VMEM],
        jax.ShapeDtypeStruct((images * rows, 128), F32),
    )
    new = lax.all_to_all(new.reshape(img_count, per_dev, 2, 2, GX, 128), "img", 0, 0, tiled=True)
    return new.transpose(1, 2, 0, 3, 4, 5).reshape(state.shape)


def solution(mesh):
    return jax.shard_map(
        local,
        mesh=mesh,
        in_specs=(P("img", None, "slab", None, None), P(), P("img")),
        out_specs=P("img", None, "slab", None, None),
        check_vma=False,
    )
```

```python
import functools

import jax
import jax.numpy as jnp
from jax import lax
from jax.experimental import pallas as pl
from jax.experimental.pallas import tpu as pltpu
from jax.sharding import PartitionSpec as P

WLEVELS = 16
KAPPA = 0.25
COUPLE = 0.3
STEP_SIZE = 0.004
EPSILON = 1e-06

F32 = jnp.float32
GX = 4
LIMIT = 14 * 1024 * 1024
MOST = 121 * 512 * 1024
UNROLL = 2


def turn(value, shift):
    return pltpu.roll(value, shift % 128, 1)


def recip(d):
    r = pltpu.reciprocal(d, approx=True)
    r = r * (2.0 - d * r)
    return r * (2.0 - d * r)


def load(ref, z):
    return [[ref[f, z, x] for x in range(GX)] for f in range(2)]


def store(ref, z, layer):
    for f in range(2):
        for x in range(GX):
            ref[f, z, x] = layer[f][x]


def each(fn, *layers):
    return [[fn(*(layer[f][x] for layer in layers)) for x in range(GX)] for f in range(2)]


def potential(below, here, above):
    mu, half = [], []
    for f in range(2):
        mu.append([])
        half.append([])
        for x in range(GX):
            phi = here[f][x]
            around = below[f][x] + above[f][x]
            around = around + (here[f][(x + 1) % GX] + here[f][(x - 1) % GX])
            around = around + (turn(phi, 1) + turn(phi, -1))
            square = phi * phi
            mu[f].append(phi * (square + (6.0 * KAPPA - 1.0)) + COUPLE * here[1 - f][x] - KAPPA * around)
            half[f].append(0.25 + 0.5 * recip(1.0 + square))
    return mu, half


def face(mu, half, mu_up, half_up):
    return each(lambda p, h, q, k: (h + k) * (q - p), mu, half, mu_up, half_up)


def outflow(mu, half, lower, upper):
    layer = []
    for f in range(2):
        p, h = mu[f], half[f]
        side = [(h[x] + h[(x + 1) % GX]) * (p[(x + 1) % GX] - p[x]) for x in range(GX)]
        along = [(h[x] + turn(h[x], -1)) * (turn(p[x], -1) - p[x]) for x in range(GX)]
        layer.append(
            [
                (side[x] - side[x - 1]) + (along[x] - turn(along[x], 1)) + (upper[f][x] - lower[f][x])
                for x in range(GX)
            ]
        )
    return layer


def drift_kernel(depth, body, fields):
    mu, half, own, kept = (fields.at[i] for i in range(4))
    for z in (0, depth - 1):
        store(kept, z, load(body, z))

    def first_fields(z, carry):
        here = load(body, z)
        store(kept, z, here)
        p, h = potential(load(body, z - 1), here, load(body, z + 1))
        store(mu, z, p)
        store(half, z, h)
        return carry

    lax.fori_loop(1, depth - 1, first_fields, 0, unroll=3)

    def flux(z, lower):
        p, h = load(mu, z), load(half, z)
        upper = face(p, h, load(mu, z + 1), load(half, z + 1))
        store(own, z, outflow(p, h, lower, upper))
        return upper

    first = face(load(mu, 1), load(half, 1), load(mu, 2), load(half, 2))
    lax.fori_loop(2, depth - 2, flux, first, unroll=4)


def rim(depth, phi, known, low_open, high_open, reach):
    fields = {}
    for z in [*range(-reach, 1), *range(depth - 1, depth + reach)]:
        fields[z] = potential(phi(z - 1), phi(z), phi(z + 1))
    for z in (1, 2, depth - 3, depth - 2):
        fields[z] = known(z)
    faces, drifts = {}, {}
    for z in [*range(-reach, 2), *range(depth - 3, depth + reach - 1)]:
        faces[z] = face(*fields[z], *fields[z + 1])
    faces[-1] = each(lambda v: v * low_open, faces[-1])
    faces[depth - 1] = each(lambda v: v * high_open, faces[depth - 1])
    for z in [*range(1 - reach, 2), *range(depth - 2, depth + reach - 1)]:
        drifts[z] = outflow(*fields[z], faces[z - 1], faces[z])
    return fields, drifts


def ends_open():
    rank = lax.axis_index("slab")
    low = jnp.where(rank > 0, 1.0, 0.0).astype(F32)
    high = jnp.where(rank < lax.axis_size("slab") - 1, 1.0, 0.0).astype(F32)
    return low, high


def even(axis):
    return 1 - lax.axis_index(axis) % 2


def neighbours(here, before, after, f, z, x, rows):
    index = (f * rows + (z + 2)) * GX + x
    sub = lax.broadcasted_iota(jnp.int32, (8, 128), 0)
    prev = jnp.where(sub == 0, before[pl.ds(index, 1), :], pltpu.roll(here, 1, 0))
    following = jnp.where(sub == 7, after[pl.ds(index, 1), :], pltpu.roll(here, 7, 0))
    return prev, following


def fetch(pairs, sems):
    copies = [pltpu.make_async_copy(source, target, sems.at[i]) for i, (source, target) in enumerate(pairs)]
    for copy in copies:
        copy.start()

    def wait():
        for copy in copies:
            copy.wait()

    return wait


def arrivals(side_a, side_b, image_a, image_b, side, image, sems):
    slab, img = even("slab"), even("img")
    return fetch(
        [
            (side_a, side.at[slab]),
            (side_b, side.at[1 - slab]),
            (image_a, image.at[img]),
            (image_b, image.at[1 - img]),
        ],
        sems,
    )


def layer_of(depth, body, side):
    low_open, high_open = ends_open()

    def phi(z):
        if z < 0:
            return each(lambda v: jnp.where(low_open > 0.0, v, 0.0), load(side.at[0], z + 4))
        if z >= depth:
            return each(lambda v: jnp.where(high_open > 0.0, v, 0.0), load(side.at[1], z - depth))
        return load(body, z)

    return phi


def sums_kernel(depth, side_a, side_b, image_a, image_b, fields, sums, side, image, sems):
    arrived = arrivals(side_a, side_b, image_a, image_b, side, image, sems)
    mu, half, own, body = (fields.at[i] for i in range(4))

    def squares(z, kept):
        one, two = jnp.zeros((8, 128), F32), jnp.zeros((8, 128), F32)
        for x in range(GX):
            one = one + own[0, z, x] * own[0, z, x]
            two = two + own[1, z, x] * own[1, z, x]
        return kept + (one + two)

    kept = lax.fori_loop(2, depth - 2, squares, jnp.zeros((8, 128), F32), unroll=4)
    arrived()
    _, drifts = rim(depth, layer_of(depth, body, side), lambda z: (load(mu, z), load(half, z)), *ends_open(), 1)
    for z in (0, 1, depth - 2, depth - 1):
        for f in range(2):
            for x in range(GX):
                kept = kept + drifts[z][f][x] * drifts[z][f][x]

    def step(z, acc):
        for f in range(2):
            for x in range(GX):
                prev, following = neighbours(body[f, z, x], image.at[0], image.at[1], f, z, x, depth + 4)
                d = following - prev
                acc = acc + d * d
        return acc

    acc = lax.fori_loop(0, depth, step, jnp.zeros((8, 128), F32), unroll=4)
    sub = lax.broadcasted_iota(jnp.int32, (8, 128), 0)
    lane = lax.broadcasted_iota(jnp.int32, (8, 128), 1)
    drift_sq = jnp.sum(kept, axis=1, keepdims=True)
    tangent_sq = jnp.sum(acc, axis=1, keepdims=True)
    row = jnp.where(lane == sub, drift_sq, jnp.where(lane == sub + 8, tangent_sq, 0.0))
    sums[...] = jnp.broadcast_to(jnp.sum(row, axis=0, keepdims=True), sums.shape)


def rim_layers(depth):
    fields = (-2, -1, 0, depth - 1, depth, depth + 1)
    drifts = (-2, -1, 0, 1, depth - 2, depth - 1, depth, depth + 1)
    return {z: i for i, z in enumerate(fields)}, {z: i for i, z in enumerate(drifts)}


def prepare_kernel(depth, side_a, side_b, image_a, image_b, fields, diff, both, rim_mu, rim_half, rim_own, *scratch):
    side, image, sems, body, ends, more = scratch
    arrived = arrivals(side_a, side_b, image_a, image_b, side, image, sems)
    pairs = [(fields.at[3], body)]
    for i in range(2):
        pairs.append((fields.at[i, :, pl.ds(1, 2)], ends.at[i, :, pl.ds(0, 2)]))
        pairs.append((fields.at[i, :, pl.ds(depth - 3, 2)], ends.at[i, :, pl.ds(2, 2)]))
    fetch(pairs, more)()
    arrived()
    place = {1: 0, 2: 1, depth - 3: 2, depth - 2: 3}
    phi = layer_of(depth, body, side)
    known, drifts = rim(depth, phi, lambda z: (load(ends.at[0], place[z]), load(ends.at[1], place[z])), *ends_open(), 3)
    slot, drift_slot = rim_layers(depth)
    for z, i in slot.items():
        store(rim_mu, i, known[z][0])
        store(rim_half, i, known[z][1])
    for z, i in drift_slot.items():
        store(rim_own, i, drifts[z])

    def images(z, here):
        for f in range(2):
            for x in range(GX):
                prev, following = neighbours(here[f][x], image.at[0], image.at[1], f, z, x, depth + 4)
                diff[f, z + 2, x] = following - prev
                both[f, z + 2, x] = following + prev

    for z in (-2, -1, depth, depth + 1):
        images(z, phi(z))

    def inside(z, carry):
        images(z, load(body, z))
        return carry

    lax.fori_loop(0, depth, inside, 0, unroll=4)


def update_kernel(depth, images, given, diff_given, both_given, rim_mu_given, rim_half_given, rim_own_given, *refs):
    sums_given, level, out, m_ref, bar, inner, fields, diff, both, rim_mu, rim_half, rim_own, sums, sems = refs
    sums_here = fetch([(sums_given, sums)], sems.at[5])
    cut = depth // 4
    parts = [(2, cut), (cut, depth - 2)]
    rim_here = fetch(
        [
            (rim_own_given, rim_own),
            (diff_given.at[:, pl.ds(0, 4)], diff.at[:, pl.ds(0, 4)]),
            (diff_given.at[:, pl.ds(depth, 4)], diff.at[:, pl.ds(depth, 4)]),
        ],
        sems.at[0],
    )
    parts_here = []
    for i, (low, high) in enumerate(parts):
        own_part, diff_part = pl.ds(low, high - low), pl.ds(low + 2, high - low)
        parts_here.append(
            fetch(
                [
                    (given.at[2, :, own_part], fields.at[2, :, own_part]),
                    (diff_given.at[:, diff_part], diff.at[:, diff_part]),
                ],
                sems.at[1 + i],
            )
        )
    flux_here = fetch(
        [
            (rim_mu_given, rim_mu),
            (rim_half_given, rim_half),
            (given.at[0], fields.at[0]),
            (given.at[1], fields.at[1]),
        ],
        sems.at[3],
    )
    rest_here = fetch([(given.at[3], fields.at[3]), (both_given, both)], sems.at[4])
    mu, half, own, body = (fields.at[i] for i in range(4))
    slot, drift_slot = rim_layers(depth)
    sub = lax.broadcasted_iota(jnp.int32, (8, 128), 0)
    lane = lax.broadcasted_iota(jnp.int32, (8, 128), 1)
    sums_here()
    added = jnp.sum(sums[...], axis=0, keepdims=True)
    drift_sq = jnp.sum(jnp.where(lane == sub, added, 0.0), axis=1, keepdims=True)
    tangent_sq = jnp.sum(jnp.where(lane == sub + 8, added, 0.0), axis=1, keepdims=True)
    rate = (images - 1) / 2.0
    scale = jnp.sqrt(drift_sq) / jnp.sqrt(tangent_sq * (rate * rate) + EPSILON)
    by_tangent = jnp.broadcast_to(scale * rate, (8, 128))
    by_second = jnp.broadcast_to(scale * scale * float((images - 1) ** 2), (8, 128))
    index = lax.axis_index("img") * 8 + sub
    step_size = jnp.where((index > 0) & (index < images - 1), STEP_SIZE, 0.0).astype(F32)
    low_open, high_open = ends_open()
    weight = jnp.zeros((8, 128), F32)
    for i in range(8):
        weight = jnp.where(sub == i, level[i].astype(F32), weight)
    weight = (weight + 1.0) / (WLEVELS + 1.0)

    def momentum(z, drift):
        store(m_ref, z + 2, each(lambda d, b: by_tangent * d - b, load(diff, z + 2), drift))

    rim_here()
    for z, i in drift_slot.items():
        momentum(z, load(rim_own, i))

    def inside(z, carry):
        momentum(z, load(own, z))
        return carry

    for (first, last), here in zip(parts, parts_here):
        here()
        lax.fori_loop(first, last, inside, 0, unroll=2)
    flux_here()

    def known(z):
        if isinstance(z, int) and z in slot:
            return load(rim_mu, slot[z]), load(rim_half, slot[z])
        return load(mu, z), load(half, z)

    def pair(z, up):
        (p, h), (q, k) = known(z), known(up)
        m, n = load(m_ref, z + 2), load(m_ref, up + 2)
        g = each(lambda a, b, c, d: (a + b) * (d - c), h, k, m, n)
        return g, each(lambda a, b, c, d: (b - a) * (d - c), p, q, m, n)

    def adjoint(z, lower, upper, is_open=None):
        p, h = known(z)
        m = load(m_ref, z + 2)
        for f in range(2):
            side = []
            for x in range(GX):
                n = (x + 1) % GX
                dm = m[f][n] - m[f][x]
                side.append(((h[f][x] + h[f][n]) * dm, dm * (p[f][n] - p[f][x])))
            for x in range(GX):
                dm = turn(m[f][x], -1) - m[f][x]
                g_y = (h[f][x] + turn(h[f][x], -1)) * dm
                q_y = dm * (turn(p[f][x], -1) - p[f][x])
                g = (side[x][0] - side[x - 1][0]) + (g_y - turn(g_y, 1)) + (upper[0][f][x] - lower[0][f][x])
                q = (side[x][1] + side[x - 1][1]) + (q_y + turn(q_y, 1)) + (upper[1][f][x] + lower[1][f][x])
                bar[f, z + 1, x] = g if is_open is None else g * is_open
                inner[f, z + 1, x] = q

    def shut(faces, is_open):
        return tuple(each(lambda v: v * is_open, layer) for layer in faces)

    faces = pair(-2, -1)
    upper = shut(pair(-1, 0), low_open)
    adjoint(-1, faces, upper, low_open)
    faces, upper = upper, pair(0, 1)
    adjoint(0, faces, upper)

    def within(z, lower):
        upper = pair(z, z + 1)
        adjoint(z, lower, upper)
        return upper

    faces = lax.fori_loop(1, depth - 2, within, upper, unroll=2)
    upper = pair(depth - 2, depth - 1)
    adjoint(depth - 2, faces, upper)
    faces, upper = upper, shut(pair(depth - 1, depth), high_open)
    adjoint(depth - 1, faces, upper)
    adjoint(depth, upper, pair(depth, depth + 1), high_open)

    def finish(r, carry):
        for zz in range(2):
            z = 2 * r + zz
            _, h = known(z)
            for f in range(2):
                g = [bar[f, z + 1, x] for x in range(GX)]
                for x in range(GX):
                    phi = body[f, z, x]
                    around = bar[f, z, x] + bar[f, z + 2, x]
                    around = around + (g[(x + 1) % GX] + g[(x - 1) % GX])
                    around = around + (turn(g[x], 1) + turn(g[x], -1))
                    inverse = 2.0 * h[f][x] - 0.5
                    pulled = phi * (inverse * inverse) * inner[f, z + 1, x]
                    pulled = pulled + (3.0 * (phi * phi) + (6.0 * KAPPA - 1.0)) * g[x]
                    pulled = pulled + COUPLE * bar[1 - f, z + 1, x] - KAPPA * around
                    second = both[f, z + 2, x] - 2.0 * phi
                    new = phi + step_size * (by_second * second + pulled)
                    out[r, pl.ds((f * 2 + zz) * GX + x, 8, stride=4 * GX), :] = new
        out[r, pl.ds(32 * GX, 8), :] = weight
        return carry

    rest_here()
    finish(0, 0)
    lax.fori_loop(1, depth // 2 - 1, finish, 0, unroll=UNROLL)
    finish(depth // 2 - 1, 0)


def mix_kernel(images, rows, starts, got, out):
    block = (rows + 1) * 8

    def step(j, carry):
        a = pl.multiple_of(starts[j], 8)
        b = pl.multiple_of(starts[images + j], 8)
        w = got[pl.ds((j // 8) * block + rows * 8 + j % 8, 1), :]
        for part in range(0, rows, 8):
            one, two = got[pl.ds(a + part, 8), :], got[pl.ds(b + part, 8), :]
            out[pl.ds(pl.multiple_of(j * rows + part, 8), 8), :] = w * one + (1.0 - w) * two
        return carry

    lax.fori_loop(0, images, step, 0, unroll=8)


ANY = pl.BlockSpec(memory_space=pl.ANY)
VMEM = pl.BlockSpec(memory_space=pltpu.VMEM)
SMEM = pl.BlockSpec(memory_space=pltpu.SMEM)


def call(kernel, ins, in_specs, outs, scratch=(), flops=0, moved=0, limit=LIMIT):
    return pl.pallas_call(
        kernel,
        in_specs=in_specs,
        out_specs=jax.tree.map(lambda _: VMEM, outs),
        out_shape=outs,
        scratch_shapes=list(scratch),
        compiler_params=pltpu.CompilerParams(vmem_limit_bytes=limit),
        cost_estimate=pl.CostEstimate(flops=flops, bytes_accessed=moved, transcendentals=0),
    )(*ins)


def swaps(count):
    near = [(i, i ^ 1) for i in range(count)]
    far = [pair for i in range(1, count, 2) for pair in ((i, (i + 1) % count), ((i + 1) % count, i))]
    return near, far


def local(state, sources, weight_index):
    img_count, slab_count = lax.axis_size("img"), lax.axis_size("slab")
    img_rank, slab_rank = lax.axis_index("img"), lax.axis_index("slab")
    per_dev, _, depth, _, _ = state.shape
    images = per_dev * img_count
    even_img, even_slab = img_rank % 2 == 0, slab_rank % 2 == 0

    near, far = swaps(slab_count)

    top = state[:, :, depth - 4 :].transpose(1, 2, 3, 0, 4)
    bottom = state[:, :, :4].transpose(1, 2, 3, 0, 4)
    side_a = lax.ppermute(jnp.where(even_slab, top, bottom), "slab", near)
    side_b = lax.ppermute(jnp.where(even_slab, bottom, top), "slab", far)
    body = lax.optimization_barrier(state).transpose(1, 2, 3, 0, 4)
    side_a, side_b, body = lax.optimization_barrier((side_a, side_b, body))
    fields = call(
        functools.partial(drift_kernel, depth),
        (body,),
        [VMEM],
        jax.ShapeDtypeStruct((4, *body.shape), F32),
        flops=16_000_000,
        moved=4_000_000,
    )

    low, high = jnp.where(even_slab, side_b, side_a)[:, 2:], jnp.where(even_slab, side_a, side_b)[:, :2]
    ends = [
        jnp.concatenate([low[:, :, :, i], state[i], high[:, :, :, i]], axis=1).reshape(-1, 128)
        for i in (0, per_dev - 1)
    ]
    near, far = swaps(img_count)
    image_a = lax.ppermute(jnp.where(even_img, ends[1], ends[0]), "img", near)
    image_b = lax.ppermute(jnp.where(even_img, ends[0], ends[1]), "img", far)

    def layers(count):
        return (2, count, GX, 8, 128)

    brought = [
        pltpu.VMEM((2, *layers(4)), F32),
        pltpu.VMEM((2, *image_a.shape), F32),
        pltpu.SemaphoreType.DMA((4,)),
    ]
    around = (side_a, side_b, image_a, image_b, fields)
    sums = call(
        functools.partial(sums_kernel, depth),
        around,
        [ANY] * 4 + [VMEM],
        jax.ShapeDtypeStruct((slab_count, 128), F32),
        brought,
    )
    sums = lax.all_to_all(sums, "slab", 0, 0, tiled=True)
    wide = layers(depth + 4)
    prepared = call(
        functools.partial(prepare_kernel, depth),
        around,
        [ANY] * 5,
        [jax.ShapeDtypeStruct(shape, F32) for shape in (wide, wide, layers(6), layers(6), layers(8))],
        brought
        + [pltpu.VMEM(layers(depth), F32), pltpu.VMEM((2, *layers(4)), F32), pltpu.SemaphoreType.DMA((5,))],
        flops=8_000_000,
        moved=4_000_000,
        limit=MOST,
    )
    rows = 4 * GX
    updated = call(
        functools.partial(update_kernel, depth, images),
        (fields, *prepared, sums, weight_index),
        [ANY] * 7 + [SMEM],
        jax.ShapeDtypeStruct((depth // 2, (rows + 1) * 8, 128), F32),
        [pltpu.VMEM(wide, F32)]
        + [pltpu.VMEM(layers(depth + 2), F32)] * 2
        + [pltpu.VMEM(array.shape, F32) for array in (fields, *prepared, sums)]
        + [pltpu.SemaphoreType.DMA((6, 4))],
        limit=MOST,
    )
    got = lax.all_to_all(updated, "img", 0, 0, tiled=True)
    starts = (sources // per_dev) * ((rows + 1) * 8) + (sources % per_dev) * rows
    new = call(
        functools.partial(mix_kernel, images, rows),
        (starts.T.reshape(-1), got.reshape(-1, 128)),
        [SMEM, VMEM],
        jax.ShapeDtypeStruct((images * rows, 128), F32),
    )
    new = lax.all_to_all(new.reshape(img_count, per_dev, 2, 2, GX, 128), "img", 0, 0, tiled=True)
    return new.transpose(1, 2, 0, 3, 4, 5).reshape(state.shape)


def solution(mesh):
    return jax.shard_map(
        local,
        mesh=mesh,
        in_specs=(P("img", None, "slab", None, None), P(), P("img")),
        out_specs=P("img", None, "slab", None, None),
        check_vma=False,
    )
```
